32 devices in a mesh: groups: 2 (over y), slab: 4 (over z), sub: 4 (over x, core).
Axes of the slice: x: 2, y: 2, z: 4, core: 2. Of those that a mesh axis runs over, the one named last changes fastest.
Arguments:
- blocks: bfloat16 [512, 7, 128, 128], P(('groups', 'slab', 'sub')), parts along dimension 0, may hold values from -6 to 6
- prolong: bfloat16 [512, 32, 128], P(('groups', 'slab', 'sub')), parts along dimension 0, may hold values from -0.5 to 0.5
- columns: int32 [512, 7], P(('groups', 'slab', 'sub')), parts along dimension 0, may hold values from 0 to 255, as said below
- live: int32 [512, 7], P(('groups', 'slab', 'sub')), parts along dimension 0, may hold values from 0 to 1, as said below
- slots: int32 [512, 7], P(('groups', 'slab', 'sub')), parts along dimension 0, may hold values from 0 to 7
- coarse_of: int32 [512], P(('groups', 'slab', 'sub')), parts along dimension 0, may hold values from 0 to 63, as said below
Outputs:
- coarse: float32 [128, 32, 256], P(('groups', 'slab', 'sub')), parts along dimension 0
The draws below stay inside these ranges and needn't reach their ends.
There are 2 independent parts, one for each index of `groups`. The reference program is written for one: setup_inputs(seed, part) draws one part's arguments, and reference() takes and returns one part's arrays. A program takes and returns all parts, laid end to end along the dimension named above; each array names one. Nothing has to cross between parts.
Inputs may be any that keep to these rules, and one draw needn't show every extreme that they name: columns[i, 0] = i; every column lies in the slab of block rows [s * 64, (s + 1) * 64) that holds i, or in one of the two slabs beside it. live[i, 0] = 1. coarse_of[i] lies in the coarse slab [s * 16, (s + 1) * 16) that holds i // 4, or in one of the two coarse slabs beside it.
All inputs are finite; a program needn't handle non-finite values.
Results may differ from the reference program's by a relative error of at most 0.0029.
Values may be sent and summed in bfloat16 or wider, within the bound.
A program may use at most 128 MiB of HBM per device.

```python
import jax
import jax.numpy as jnp
from jax import lax

BS = 128
CB = 32
NBR = 7
KC = 8
ROWS = 16
SLAB_ROWS = 64
SLAB_COARSE = 16
NB = 256
NC = 64


def draw_columns(key, part):
    key = jax.random.fold_in(key, 11)
    rows = jnp.arange(NB, dtype=jnp.int32)
    slab_of = rows // SLAB_ROWS
    lower = (slab_of - 1) * SLAB_ROWS
    upper = (slab_of + 2) * SLAB_ROWS
    others = jax.random.randint(key, (NB, NBR - 1), lower[:, None], upper[:, None])
    others = jnp.clip(others, 0, NB - 1)
    return jnp.concatenate([rows[:, None], others], axis=1).astype(jnp.int32)


def draw_live(key, part):
    key = jax.random.fold_in(key, 12)
    picks = jax.random.randint(key, (NB, NBR - 1), 0, 4)
    alive = (picks > 0).astype(jnp.int32)
    return jnp.concatenate([jnp.ones((NB, 1), jnp.int32), alive], axis=1)


def draw_coarse_of(key, part):
    key = jax.random.fold_in(key, 13)
    rows = jnp.arange(NB, dtype=jnp.int32)
    offset = jax.random.randint(key, (NB,), -SLAB_COARSE, SLAB_COARSE + 1)
    offset = jnp.where((rows == 0) | (rows == NB - 1), 0, offset)
    return jnp.clip(rows // 4 + offset, 0, NC - 1).astype(jnp.int32)


def with_ends(drawn, key, low, high):
    place = [jax.random.randint(jax.random.fold_in(key, axis), (), 0, length) for axis, length in enumerate(drawn.shape)]
    main_axis = drawn.shape.index(max(drawn.shape))
    next_to = place[:main_axis] + [(place[main_axis] + 1) % drawn.shape[main_axis]] + place[main_axis + 1:]
    return drawn.at[tuple(place)].set(low).at[tuple(next_to)].set(high)


def block_scale(key, dims, shards, least, top_value):
    factor_of = 1.0
    for position, blocks in shards:
        steps = jax.random.uniform(jax.random.fold_in(jax.random.fold_in(key, 6), position), (blocks,), jnp.float32, least / len(shards), top_value / len(shards))
        factor_of = factor_of * jnp.repeat(jnp.exp(steps), dims[position] // blocks).reshape((-1,) + (1,) * (len(dims) - 1 - position))
    return factor_of


def normal_values(rng, dims, deviation, limit, cuts=(), kind=jnp.bfloat16):
    loudness = block_scale(rng, dims, cuts, -0.22, 0.18) if cuts else 1.0
    array = jax.random.normal(rng, dims, jnp.float32) * deviation * loudness
    return jnp.minimum(jnp.maximum(array, -limit), limit).astype(kind)


def setup_inputs(seed: int = 0, part: int = 0) -> dict:
    arg_keys = jax.random.split(jax.random.key(seed), 7)
    part_keys = jax.random.split(jax.random.fold_in(arg_keys[6], part), 7)
    return {
        "blocks": normal_values(part_keys[0], (NB, NBR, BS, BS), 1.0, 6.0, ((0, 16),)),
        "prolong": normal_values(part_keys[1], (NB, CB, BS), BS ** -0.5, 0.5, ((0, 16),)),
        "columns": draw_columns(jax.random.fold_in(jax.random.fold_in(arg_keys[6], part), 71), part),
        "live": draw_live(jax.random.fold_in(jax.random.fold_in(arg_keys[6], part), 71), part),
        "slots": with_ends(jax.random.randint(part_keys[4], (NB, NBR), 0, KC), jax.random.fold_in(part_keys[4], 1), 0, KC - 1).astype(jnp.int32),
        "coarse_of": draw_coarse_of(jax.random.fold_in(jax.random.fold_in(arg_keys[6], part), 71), part),
    }


def reference(blocks, prolong, columns, live, slots, coarse_of):
    group_count = NB // ROWS

    def one_group(args):
        blk, cols, alive, own = args
        far = prolong[cols].astype(jnp.float32)
        applied = jnp.einsum("gkcb,gkab->gkca", far, blk.astype(jnp.float32))
        applied = lax.optimization_barrier(applied.astype(jnp.bfloat16)).astype(jnp.float32)
        term = jnp.einsum("gxa,gkca->gkxc", own.astype(jnp.float32), applied)
        return term * alive[:, :, None, None].astype(jnp.float32)

    terms = lax.map(one_group, (blocks.reshape(group_count, ROWS, NBR, BS, BS),
                                columns.reshape(group_count, ROWS, NBR),
                                live.reshape(group_count, ROWS, NBR),
                                prolong.reshape(group_count, ROWS, CB, BS)))
    target = (coarse_of[:, None].astype(jnp.int32) * KC + slots.astype(jnp.int32)).reshape(-1)
    summed = jax.ops.segment_sum(terms.reshape(NB * NBR, CB, CB), target, num_segments=NC * KC)
    return summed.reshape(NC, KC, CB, CB).transpose(0, 2, 1, 3).reshape(NC, CB, KC * CB)
```

```python
import functools

import jax
import jax.numpy as jnp
from jax import lax
from jax.experimental import pallas as pl
from jax.experimental.pallas import tpu as pltpu
from jax.sharding import PartitionSpec as P

BS = 128
CB = 32
KC = 8
CORES = 2
CHUNKS = 4
MESH = pl.DeviceIdType.MESH
NT = (((1,), (1,)), ((), ()))


def kernel(n_slab, n_sub, columns, live, slots, coarse_of, prolong, blocks, out,
           wide, blk, qs, tb, dmat, wm, mrecv, wo, sb, rbuf,
           own_sem, blk_sem, p1s, p1r, fs, fr, ms, mr, p2s, p2r):
    rows, nbr = blk.shape[0], blk.shape[1]
    n_x = n_sub // CORES
    ncr = rows // 4
    piece = ncr * CB
    slab_rows = rows * n_sub
    slab_coarse = ncr * n_sub
    z = lax.axis_index("slab")
    sub = lax.axis_index("sub")
    x, c = lax.div(sub, CORES), lax.rem(sub, CORES)
    mate = sub + 1 - 2 * c
    per = rows // CHUNKS

    def there(dz, fn):
        if dz == 0:
            fn()
        else:
            pl.when(jnp.logical_and(z + dz >= 0, z + dz < n_slab))(fn)

    def place(group, owner):
        return pl.ds((group * n_sub + owner) * rows, rows)

    own = pltpu.make_async_copy(prolong, wide.at[place(1, sub)], own_sem)
    own.start()
    loads = [
        pltpu.make_async_copy(blocks.at[pl.ds(n * per, per)], blk.at[pl.ds(n * per, per)], blk_sem.at[n])
        for n in range(CHUNKS)
    ]
    for load in loads:
        load.start()

    barrier = pltpu.get_barrier_semaphore()
    offsets = [(dz, ox) for dz in (0, -1, 1) for ox in range(n_x)]
    plane = [o for o in offsets if o != (0, 0)]

    def to_sub(ox):
        return lax.rem(x + ox, n_x) * CORES + c

    def from_sub(ox, core):
        return lax.rem(x + n_x - ox, n_x) * CORES + core

    def greet(dz, ox):
        def go():
            pl.semaphore_signal(barrier, inc=1, device_id={"slab": z + dz, "sub": to_sub(ox)},
                                device_id_type=MESH)
        return go

    pl.semaphore_signal(barrier, inc=1, device_id={"sub": mate}, device_id_type=MESH)
    for dz, ox in plane:
        there(dz, greet(dz, ox))
    ends = (z == 0).astype(jnp.int32) + (z == n_slab - 1).astype(jnp.int32)
    pl.semaphore_wait(barrier, 3 * n_x - n_x * ends)

    def p1_send(dz, ox):
        return pltpu.make_async_remote_copy(
            src_ref=prolong, dst_ref=wide.at[place(1 - dz, sub)],
            send_sem=p1s.at[dz + 1, ox], recv_sem=p1r.at[dz + 1, ox],
            device_id={"slab": z + dz, "sub": to_sub(ox)}, device_id_type=MESH)

    def p1_recv(dz, ox):
        spot = wide.at[place(1 - dz, from_sub(ox, c))]
        return pltpu.make_async_remote_copy(
            src_ref=spot, dst_ref=spot,
            send_sem=p1s.at[dz + 1, ox], recv_sem=p1r.at[dz + 1, ox],
            device_id={"slab": z, "sub": mate}, device_id_type=MESH)

    def fwd(dz, ox, core):
        spot = wide.at[place(1 - dz, from_sub(ox, core))]
        return pltpu.make_async_remote_copy(
            src_ref=prolong if (dz, ox) == (0, 0) else spot, dst_ref=spot,
            send_sem=fs.at[dz + 1, ox], recv_sem=fr.at[dz + 1, ox],
            device_id={"slab": z, "sub": mate}, device_id_type=MESH)

    for dz, ox in reversed(plane):
        there(dz, lambda dz=dz, ox=ox: p1_send(dz, ox).start())
    fwd(0, 0, c).start()

    for dz in (-1, 1):
        @pl.when(jnp.logical_not(jnp.logical_and(z - dz >= 0, z - dz < n_slab)))
        def _():
            rbuf[dz + 1] = jnp.zeros(rbuf.shape[1:], rbuf.dtype)

    shape = dmat.shape
    lane = lax.broadcasted_iota(jnp.int32, shape, 1)
    row = lax.broadcasted_iota(jnp.int32, shape, 0)
    first_coarse = (z - 1) * slab_coarse
    lane_row = lax.broadcasted_iota(jnp.int32, (1, shape[1]), 1) // CB
    ce = jnp.zeros((1, shape[1]), jnp.int32)
    for i in range(rows):
        ce = jnp.where(lane_row == i, coarse_of[i] - first_coarse, ce)
    shift = (row // piece) * (CORES * ncr) + (row % piece) // CB
    dmat[...] = jnp.where(lane % CB == row % CB, ce - shift, -(2 ** 20))

    own.wait()

    def left(i):
        mine = wide[(n_sub + sub) * rows + i]
        for k in range(nbr):
            q = jnp.dot(mine, blk[i, k], preferred_element_type=jnp.float32)
            high = q.astype(jnp.bfloat16)
            low = (q - high.astype(jnp.float32)).astype(jnp.bfloat16)
            qs[i, :CB, k * BS:(k + 1) * BS] = high
            qs[i, CB:, k * BS:(k + 1) * BS] = low

    def pass_on(dz, ox):
        def go():
            p1_recv(dz, ox).wait_recv()
            fwd(dz, ox, c).start()
        there(-dz, go)

    turns = sorted(plane, key=lambda o: (o[1] > 0 and o[0] != 0, o[1]))
    for n in range(CHUNKS):
        loads[n].wait()

        @pl.loop(0, per, unroll=per)
        def _(t):
            left(n * per + t)
        if n == CHUNKS - 2:
            for o in turns[:len(turns) // 2]:
                pass_on(*o)
    for o in turns[len(turns) // 2:]:
        pass_on(*o)
    for dz, ox in offsets:
        there(-dz, lambda dz=dz, ox=ox: fwd(dz, ox, 1 - c).wait_recv())

    first_row = (z - 1) * slab_rows

    def right(i):
        parts = []
        for k in range(nbr):
            far = wide[jnp.clip(columns[k, i] - first_row, 0, 3 * slab_rows - 1)]
            slot, alive = slots[k, i], live[k, i]
            marks = [jnp.where(slot == s, alive, 0).astype(jnp.float32).astype(jnp.bfloat16) for s in range(KC)]
            parts.append(jnp.concatenate([far * m for m in marks], axis=0))
        both = lax.dot_general(qs[i], jnp.concatenate(parts, axis=1), NT,
                               preferred_element_type=jnp.float32)
        tb[pl.ds(pl.multiple_of(i * CB, CB), CB), :] = (both[:CB] + both[CB:]).astype(jnp.bfloat16)

    @pl.loop(0, rows, unroll=4)
    def _(i):
        right(i)

    def window(group, core):
        pick = (dmat[...] == group * slab_coarse + core * ncr)
        pick = jnp.where(pick, 1.0, 0.0).astype(jnp.bfloat16)
        return jnp.dot(pick, tb[...], preferred_element_type=jnp.float32)

    def over(group):
        return pltpu.make_async_remote_copy(
            src_ref=wm.at[group], dst_ref=mrecv.at[group],
            send_sem=ms.at[group], recv_sem=mr.at[group],
            device_id={"slab": z, "sub": mate}, device_id_type=MESH)

    order = (0, 2, 1)
    for g in order:
        wm[g] = window(g, 1 - c).astype(jnp.bfloat16)
        over(g).start()
    for g in order:
        wo[g] = window(g, c)

    def p2(dz, ox):
        at = pl.ds(pl.multiple_of(lax.rem(x + ox, n_x) * piece, piece), piece)
        return pltpu.make_async_remote_copy(
            src_ref=sb.at[dz + 1, at], dst_ref=rbuf.at[dz + 1, ox],
            send_sem=p2s.at[dz + 1, ox], recv_sem=p2r.at[dz + 1, ox],
            device_id={"slab": z + dz, "sub": to_sub(ox)}, device_id_type=MESH)

    for g in order:
        over(g).wait_recv()
        total = wo[g] + mrecv[g].astype(jnp.float32)
        sb[g] = total.astype(jnp.bfloat16)
        if g == 1:
            wo[g] = total
        for ox in reversed(range(n_x)):
            if (g - 1, ox) != (0, 0):
                there(g - 1, lambda dz=g - 1, ox=ox: p2(dz, ox).start())

    for dz, ox in plane:
        there(-dz, lambda dz=dz, ox=ox: p2(dz, ox).wait_recv())
    total = wo[1, pl.ds(pl.multiple_of(x * piece, piece), piece), :]
    for dz, ox in plane:
        total = total + rbuf[dz + 1, ox].astype(jnp.float32)
    out[...] = total.reshape(out.shape)

    for g in order:
        over(g).wait_send()
    for dz, ox in plane:
        there(dz, lambda dz=dz, ox=ox: p1_send(dz, ox).wait_send())
        there(dz, lambda dz=dz, ox=ox: p2(dz, ox).wait_send())
    for dz, ox in offsets:
        there(-dz, lambda dz=dz, ox=ox: fwd(dz, ox, c).wait_send())


def body(n_slab, n_sub, blocks, prolong, columns, live, slots, coarse_of):
    rows, nbr = blocks.shape[:2]
    ncr = rows // 4
    n_x = n_sub // CORES
    half = n_x * ncr * CB
    smem = pl.BlockSpec(memory_space=pltpu.SMEM)
    hbm = pl.BlockSpec(memory_space=pltpu.HBM)
    dma = pltpu.SemaphoreType.DMA
    flops = 2 * rows * nbr * CB * BS * (BS + CB)
    return pl.pallas_call(
        functools.partial(kernel, n_slab, n_sub),
        out_shape=jax.ShapeDtypeStruct((ncr, CB, KC * CB), jnp.float32),
        in_specs=[smem] * 4 + [hbm] * 2,
        out_specs=pl.BlockSpec(memory_space=pltpu.VMEM),
        scratch_shapes=[
            pltpu.VMEM((3 * n_sub * rows, CB, BS), jnp.bfloat16),
            pltpu.VMEM((rows, nbr, BS, BS), jnp.bfloat16),
            pltpu.VMEM((rows, 2 * CB, nbr * BS), jnp.bfloat16),
            pltpu.VMEM((rows * CB, KC * CB), jnp.bfloat16),
            pltpu.VMEM((half, rows * CB), jnp.int32),
            pltpu.VMEM((3, half, KC * CB), jnp.bfloat16),
            pltpu.VMEM((3, half, KC * CB), jnp.bfloat16),
            pltpu.VMEM((3, half, KC * CB), jnp.float32),
            pltpu.VMEM((3, half, KC * CB), jnp.bfloat16),
            pltpu.VMEM((3, n_x, ncr * CB, KC * CB), jnp.bfloat16),
            dma(()), dma((CHUNKS,)),
            dma((3, n_x)), dma((3, n_x)), dma((3, n_x)), dma((3, n_x)),
            dma((3,)), dma((3,)), dma((3, n_x)), dma((3, n_x)),
        ],
        compiler_params=pltpu.CompilerParams(
            collective_id=0, has_side_effects=True, vmem_limit_bytes=63 * 2 ** 20),
        cost_estimate=pl.CostEstimate(flops=flops, bytes_accessed=2 * blocks.size, transcendentals=0),
    )(columns.T, live.T, slots.T, coarse_of, prolong, blocks)


def solution(mesh):
    rows = ("groups", "slab", "sub")
    in_specs = (
        P(rows, None, None, None), P(rows, None, None),
        P(rows, None), P(rows, None), P(rows, None), P(rows),
    )
    part = functools.partial(body, mesh.shape["slab"], mesh.shape["sub"])
    return jax.shard_map(part, mesh=mesh, in_specs=in_specs, out_specs=P(rows, None, None), check_vma=False)
```

```python
import functools

import jax
import jax.numpy as jnp
from jax import lax
from jax.experimental import pallas as pl
from jax.experimental.pallas import tpu as pltpu
from jax.sharding import PartitionSpec as P

BS = 128
CB = 32
KC = 8
CORES = 2
CHUNKS = 4
MESH = pl.DeviceIdType.MESH
NT = (((1,), (1,)), ((), ()))


def kernel(n_slab, n_sub, columns, live, slots, coarse_of, prolong, blocks, out,
           wide, blk, qs, tb, ce, picks, sb, rbuf,
           own_sem, blk_sem, p1s, p1r, fs, fr, cs, cr, ts, tr, p2s, p2r):
    rows, nbr = blk.shape[0], blk.shape[1]
    n_x = n_sub // CORES
    ncr = rows // 4
    piece = ncr * CB
    slab_rows = rows * n_sub
    slab_coarse = ncr * n_sub
    z = lax.axis_index("slab")
    sub = lax.axis_index("sub")
    x, c = lax.div(sub, CORES), lax.rem(sub, CORES)
    mate = sub + 1 - 2 * c
    per = rows // CHUNKS
    to_mate = {"device_id": {"slab": z, "sub": mate}, "device_id_type": MESH}

    def there(dz, fn):
        if dz == 0:
            fn()
        else:
            pl.when(jnp.logical_and(z + dz >= 0, z + dz < n_slab))(fn)

    def place(group, owner):
        return pl.ds((group * n_sub + owner) * rows, rows)

    own = pltpu.make_async_copy(prolong, wide.at[place(1, sub)], own_sem)
    own.start()
    loads = [
        pltpu.make_async_copy(blocks.at[pl.ds(n * per, per)], blk.at[pl.ds(n * per, per)], blk_sem.at[n])
        for n in range(CHUNKS)
    ]
    for load in loads:
        load.start()

    barrier = pltpu.get_barrier_semaphore()
    offsets = [(dz, ox) for dz in (0, -1, 1) for ox in range(n_x)]
    plane = [o for o in offsets if o != (0, 0)]

    def to_sub(ox):
        return lax.rem(x + ox, n_x) * CORES + c

    def from_sub(ox, core):
        return lax.rem(x + n_x - ox, n_x) * CORES + core

    def greet(dz, ox):
        def go():
            pl.semaphore_signal(barrier, inc=1, device_id={"slab": z + dz, "sub": to_sub(ox)},
                                device_id_type=MESH)
        return go

    pl.semaphore_signal(barrier, inc=1, device_id={"sub": mate}, device_id_type=MESH)
    for dz, ox in plane:
        there(dz, greet(dz, ox))
    ends = (z == 0).astype(jnp.int32) + (z == n_slab - 1).astype(jnp.int32)
    pl.semaphore_wait(barrier, 3 * n_x - n_x * ends)

    def spot(dz, ox, core):
        return wide.at[place(1 - dz, from_sub(ox, core))]

    def p1_send(dz, ox):
        straight = dz != 0
        return pltpu.make_async_remote_copy(
            src_ref=spot(0, ox, c) if straight and ox else prolong,
            dst_ref=spot(dz, ox, c) if straight else wide.at[place(1, sub)],
            send_sem=p1s.at[dz + 1, ox], recv_sem=p1r.at[dz + 1, ox],
            device_id={"slab": z + dz, "sub": sub if straight else to_sub(ox)}, device_id_type=MESH)

    def p1_recv(dz, ox):
        return pltpu.make_async_remote_copy(
            src_ref=spot(dz, ox, c), dst_ref=spot(dz, ox, c),
            send_sem=p1s.at[dz + 1, ox], recv_sem=p1r.at[dz + 1, ox], **to_mate)

    def fwd(dz, ox, core):
        return pltpu.make_async_remote_copy(
            src_ref=prolong if (dz, ox) == (0, 0) else spot(dz, ox, core), dst_ref=spot(dz, ox, core),
            send_sem=fs.at[dz + 1, ox], recv_sem=fr.at[dz + 1, ox], **to_mate)

    for ox in range(1, n_x):
        p1_send(0, ox).start()
    for dz in (-1, 1):
        there(dz, lambda dz=dz: p1_send(dz, 0).start())
    fwd(0, 0, c).start()

    lane_row = lax.broadcasted_iota(jnp.int32, ce.shape[1:], 1) // CB
    mine = jnp.zeros(ce.shape[1:], jnp.int32)
    for i in range(rows):
        mine = jnp.where(lane_row == i, coarse_of[i], mine)
    ce[0] = mine
    ce_copy = pltpu.make_async_remote_copy(
        src_ref=ce.at[0], dst_ref=ce.at[1], send_sem=cs, recv_sem=cr, **to_mate)
    ce_copy.start()

    for dz in (-1, 1):
        @pl.when(jnp.logical_not(jnp.logical_and(z - dz >= 0, z - dz < n_slab)))
        def _():
            rbuf[dz + 1] = jnp.zeros(rbuf.shape[1:], rbuf.dtype)

    own.wait()

    def left(i):
        mine = wide[(n_sub + sub) * rows + i]
        for k in range(nbr):
            q = jnp.dot(mine, blk[i, k], preferred_element_type=jnp.float32)
            high = q.astype(jnp.bfloat16)
            low = (q - high.astype(jnp.float32)).astype(jnp.bfloat16)
            qs[i, :CB, k * BS:(k + 1) * BS] = high
            qs[i, CB:, k * BS:(k + 1) * BS] = low

    def pass_on(dz, ox):
        def go():
            p1_recv(dz, ox).wait_recv()
            if dz == 0:
                for to in (-1, 1):
                    there(to, lambda to=to: p1_send(to, ox).start())
            fwd(dz, ox, c).start()
        there(-dz, go)

    def rows_left(n):
        loads[n].wait()

        @pl.loop(0, per, unroll=per)
        def _(t):
            left(n * per + t)

    for n in range(CHUNKS // 2):
        rows_left(n)
    for ox in range(1, n_x):
        pass_on(0, ox)
    for n in range(CHUNKS // 2, CHUNKS):
        rows_left(n)
    for dz in (-1, 1):
        pass_on(dz, 0)

    ce_copy.wait_recv()
    wide_ce = jnp.concatenate([jnp.broadcast_to(ce[h, :1], (CB, rows * CB)) for h in range(CORES)], axis=1)
    lane = lax.broadcasted_iota(jnp.int32, wide_ce.shape, 1)
    row = lax.broadcasted_iota(jnp.int32, wide_ce.shape, 0)
    wide_ce = jnp.where(lane % CB == row, wide_ce - (z - 1) * slab_coarse, -(2 ** 20))
    for g in range(3):
        for t in range(n_x):
            for q in range(ncr):
                pick = wide_ce == g * slab_coarse + (t * CORES + c) * ncr + q
                picks[g, t * piece + q * CB:t * piece + (q + 1) * CB, :] = (
                    jnp.where(pick, 1.0, 0.0).astype(jnp.bfloat16))

    for ox in range(1, n_x):
        for dz in (-1, 1):
            pass_on(dz, ox)
    for dz, ox in offsets:
        there(-dz, lambda dz=dz, ox=ox: fwd(dz, ox, 1 - c).wait_recv())

    first_row = (z - 1) * slab_rows
    lane_slot = lax.broadcasted_iota(jnp.int32, (CB, KC * CB), 1) // CB

    def right(i):
        total = jnp.zeros((CB, KC * CB), jnp.float32)
        for k in range(nbr):
            far = wide[jnp.clip(columns[k, i] - first_row, 0, 3 * slab_rows - 1)]
            both = lax.dot_general(qs[i, :, k * BS:(k + 1) * BS], jnp.concatenate([far] * KC, axis=0), NT,
                                   preferred_element_type=jnp.float32)
            slot = jnp.where(live[k, i] != 0, slots[k, i], -1)
            total += jnp.where(lane_slot == slot, both[:CB] + both[CB:], 0.0)
        tb[0, pl.ds(pl.multiple_of(i * CB, CB), CB), :] = total.astype(jnp.bfloat16)

    def share(n):
        at = pl.ds(n * per * CB, per * CB)
        return pltpu.make_async_remote_copy(
            src_ref=tb.at[0, at], dst_ref=tb.at[1, at], send_sem=ts.at[n], recv_sem=tr.at[n], **to_mate)

    for n in range(CHUNKS):
        @pl.loop(0, per, unroll=per)
        def _(t):
            right(n * per + t)
        share(n).start()
    for n in range(CHUNKS):
        share(n).wait_recv()

    def p2(dz, ox):
        at = pl.ds(pl.multiple_of(lax.rem(x + ox, n_x) * piece, piece), piece)
        return pltpu.make_async_remote_copy(
            src_ref=sb.at[dz + 1, at], dst_ref=rbuf.at[dz + 1, ox],
            send_sem=p2s.at[dz + 1, ox], recv_sem=p2r.at[dz + 1, ox],
            device_id={"slab": z + dz, "sub": to_sub(ox)}, device_id_type=MESH)

    terms = tb[...].reshape(CORES * rows * CB, KC * CB)
    for g in (0, 2, 1):
        sb[g] = jnp.dot(picks[g], terms, preferred_element_type=jnp.float32).astype(jnp.bfloat16)
        for ox in reversed(range(n_x)):
            if (g - 1, ox) != (0, 0):
                there(g - 1, lambda dz=g - 1, ox=ox: p2(dz, ox).start())

    total = sb[1, pl.ds(pl.multiple_of(x * piece, piece), piece), :].astype(jnp.float32)
    for dz, ox in plane:
        there(-dz, lambda dz=dz, ox=ox: p2(dz, ox).wait_recv())
    for dz, ox in plane:
        total = total + rbuf[dz + 1, ox].astype(jnp.float32)
    out[...] = total.reshape(out.shape)

    ce_copy.wait_send()
    for n in range(CHUNKS):
        share(n).wait_send()
    for dz, ox in plane:
        there(dz, lambda dz=dz, ox=ox: p1_send(dz, ox).wait_send())
        there(dz, lambda dz=dz, ox=ox: p2(dz, ox).wait_send())
    for dz, ox in offsets:
        there(-dz, lambda dz=dz, ox=ox: fwd(dz, ox, c).wait_send())


def body(n_slab, n_sub, blocks, prolong, columns, live, slots, coarse_of):
    rows, nbr = blocks.shape[:2]
    ncr = rows // 4
    n_x = n_sub // CORES
    half = n_x * ncr * CB
    smem = pl.BlockSpec(memory_space=pltpu.SMEM)
    hbm = pl.BlockSpec(memory_space=pltpu.HBM)
    dma = pltpu.SemaphoreType.DMA
    flops = 2 * rows * nbr * CB * BS * (BS + CB)
    return pl.pallas_call(
        functools.partial(kernel, n_slab, n_sub),
        out_shape=jax.ShapeDtypeStruct((ncr, CB, KC * CB), jnp.float32),
        in_specs=[smem] * 4 + [hbm] * 2,
        out_specs=pl.BlockSpec(memory_space=pltpu.VMEM),
        scratch_shapes=[
            pltpu.VMEM((3 * n_sub * rows, CB, BS), jnp.bfloat16),
            pltpu.VMEM((rows, nbr, BS, BS), jnp.bfloat16),
            pltpu.VMEM((rows, 2 * CB, nbr * BS), jnp.bfloat16),
            pltpu.VMEM((CORES, rows * CB, KC * CB), jnp.bfloat16),
            pltpu.VMEM((CORES, 8, rows * CB), jnp.int32),
            pltpu.VMEM((3, half, CORES * rows * CB), jnp.bfloat16),
            pltpu.VMEM((3, half, KC * CB), jnp.bfloat16),
            pltpu.VMEM((3, n_x, ncr * CB, KC * CB), jnp.bfloat16),
            dma(()), dma((CHUNKS,)),
            dma((3, n_x)), dma((3, n_x)), dma((3, n_x)), dma((3, n_x)),
            dma(()), dma(()), dma((CHUNKS,)), dma((CHUNKS,)), dma((3, n_x)), dma((3, n_x)),
        ],
        compiler_params=pltpu.CompilerParams(
            collective_id=0, has_side_effects=True, vmem_limit_bytes=63 * 2 ** 20),
        cost_estimate=pl.CostEstimate(flops=flops, bytes_accessed=2 * blocks.size, transcendentals=0),
    )(columns.T, live.T, slots.T, coarse_of, prolong, blocks)


def solution(mesh):
    rows = ("groups", "slab", "sub")
    in_specs = (
        P(rows, None, None, None), P(rows, None, None),
        P(rows, None), P(rows, None), P(rows, None), P(rows),
    )
    part = functools.partial(body, mesh.shape["slab"], mesh.shape["sub"])
    return jax.shard_map(part, mesh=mesh, in_specs=in_specs, out_specs=P(rows, None, None), check_vma=False)
```

```python
import functools

import jax
import jax.numpy as jnp
from jax import lax
from jax.experimental import pallas as pl
from jax.experimental.pallas import tpu as pltpu
from jax.sharding import PartitionSpec as P

BS = 128
CB = 32
KC = 8
CORES = 2
CHUNKS = 4
HALVES = 2
DIRECT = 0
SHARES = 1
MESH = pl.DeviceIdType.MESH
NT = (((1,), (1,)), ((), ()))


def kernel(n_slab, n_sub, columns_in, live_in, slots_in, coarse_of_in, prolong, blocks, out,
           columns, live, slots, coarse_of, wide, blk, qs, sel, th, tb, ce, picks, wo, sb, rbuf,
           int_sem, own_sem, blk_sem, p1s, p1r, fs, fr, cs, cr, ts, tr, p2s, p2r):
    rows, nbr = blk.shape[0], blk.shape[1]
    n_x = n_sub // CORES
    ncr = rows // 4
    piece = ncr * CB
    slab_rows = rows * n_sub
    slab_coarse = ncr * n_sub
    z = lax.axis_index("slab")
    sub = lax.axis_index("sub")
    x, c = lax.div(sub, CORES), lax.rem(sub, CORES)
    mate = sub + 1 - 2 * c
    per = rows // CHUNKS
    to_mate = {"device_id": {"slab": z, "sub": mate}, "device_id_type": MESH}

    def there(dz, fn):
        if dz == 0:
            fn()
        else:
            pl.when(jnp.logical_and(z + dz >= 0, z + dz < n_slab))(fn)

    part = rows // HALVES

    def place(group, owner, h=None):
        first = (group * n_sub + owner) * rows
        return pl.ds(first, rows) if h is None else pl.ds(first + h * part, part)

    own = pltpu.make_async_copy(prolong, wide.at[place(1, sub)], own_sem)
    own.start()
    loads = [
        pltpu.make_async_copy(blocks.at[pl.ds(n * per, per)], blk.at[pl.ds(n * per, per)], blk_sem.at[n])
        for n in range(CHUNKS)
    ]
    for load in loads:
        load.start()
    ints = [
        pltpu.make_async_copy(given, kept, int_sem.at[n])
        for n, (given, kept) in enumerate(((coarse_of_in, coarse_of), (slots_in, slots), (live_in, live),
                                           (columns_in, columns)))
    ]
    for copy in ints:
        copy.start()

    barrier = pltpu.get_barrier_semaphore()
    offsets = [(dz, ox) for dz in (0, -1, 1) for ox in range(n_x)]
    plane = [o for o in offsets if o != (0, 0)]

    def to_sub(ox):
        return lax.rem(x + ox, n_x) * CORES + c

    def from_sub(ox, core):
        return lax.rem(x + n_x - ox, n_x) * CORES + core

    def greet(dz, ox):
        def go():
            pl.semaphore_signal(barrier, inc=1, device_id={"slab": z + dz, "sub": to_sub(ox)},
                                device_id_type=MESH)
        return go

    pl.semaphore_signal(barrier, inc=1, device_id={"sub": mate}, device_id_type=MESH)
    for dz, ox in plane:
        there(dz, greet(dz, ox))
    ends = (z == 0).astype(jnp.int32) + (z == n_slab - 1).astype(jnp.int32)
    pl.semaphore_wait(barrier, 3 * n_x - n_x * ends)

    def spot(dz, ox, core, h):
        return wide.at[place(1 - dz, from_sub(ox, core), h)]

    def p1_send(dz, ox, h):
        passed = dz != 0 and ox != 0 and h < HALVES - DIRECT
        return pltpu.make_async_remote_copy(
            src_ref=spot(0, ox, c, h) if passed else prolong.at[pl.ds(h * part, part)],
            dst_ref=spot(dz, ox, c, h) if passed else wide.at[place(1 - dz, sub, h)],
            send_sem=p1s.at[dz + 1, ox, h], recv_sem=p1r.at[dz + 1, ox, h],
            device_id={"slab": z + dz, "sub": sub if passed else to_sub(ox)}, device_id_type=MESH)

    def p1_recv(dz, ox, h):
        return pltpu.make_async_remote_copy(
            src_ref=spot(dz, ox, c, h), dst_ref=spot(dz, ox, c, h),
            send_sem=p1s.at[dz + 1, ox, h], recv_sem=p1r.at[dz + 1, ox, h], **to_mate)

    def fwd(dz, ox, core, h):
        return pltpu.make_async_remote_copy(
            src_ref=prolong.at[pl.ds(h * part, part)] if (dz, ox) == (0, 0) else spot(dz, ox, core, h),
            dst_ref=spot(dz, ox, core, h),
            send_sem=fs.at[dz + 1, ox, h], recv_sem=fr.at[dz + 1, ox, h], **to_mate)

    halves = range(HALVES)
    for h in halves:
        for ox in range(1, n_x):
            p1_send(0, ox, h).start()
        for dz in (-1, 1):
            there(dz, lambda dz=dz, h=h: p1_send(dz, 0, h).start())
    for h in halves[HALVES - DIRECT:]:
        for ox in range(1, n_x):
            for dz in (-1, 1):
                there(dz, lambda dz=dz, ox=ox, h=h: p1_send(dz, ox, h).start())
    for h in halves:
        fwd(0, 0, c, h).start()

    lane_row = lax.broadcasted_iota(jnp.int32, ce.shape[1:], 1) // CB
    mine = jnp.zeros(ce.shape[1:], jnp.int32)
    for copy in ints:
        copy.wait()
    for i in range(rows):
        mine = jnp.where(lane_row == i, coarse_of[i], mine)
    ce[0] = mine
    ce_copy = pltpu.make_async_remote_copy(
        src_ref=ce.at[0], dst_ref=ce.at[1], send_sem=cs, recv_sem=cr, **to_mate)
    ce_copy.start()

    for dz in (-1, 1):
        @pl.when(jnp.logical_not(jnp.logical_and(z - dz >= 0, z - dz < n_slab)))
        def _():
            rbuf[dz + 1] = jnp.zeros(rbuf.shape[1:], rbuf.dtype)

    own.wait()

    def left(i):
        mine = wide[(n_sub + sub) * rows + i]
        for k in range(nbr):
            q = jnp.dot(mine, blk[i, k], preferred_element_type=jnp.float32)
            high = q.astype(jnp.bfloat16)
            low = (q - high.astype(jnp.float32)).astype(jnp.bfloat16)
            qs[i, k * CB:(k + 1) * CB, :BS] = high
            qs[i, k * CB:(k + 1) * CB, BS:] = low

    def pass_on(dz, ox, h):
        def go():
            p1_recv(dz, ox, h).wait_recv()
            if dz == 0 and h < HALVES - DIRECT:
                for to in (-1, 1):
                    there(to, lambda to=to: p1_send(to, ox, h).start())
            fwd(dz, ox, c, h).start()
        there(-dz, go)

    def rows_left(n):
        loads[n].wait()

        @pl.loop(0, per, unroll=per)
        def _(t):
            left(n * per + t)

    for n in range(CHUNKS // 2):
        rows_left(n)
    for ox in range(1, n_x):
        pass_on(0, ox, 0)
    rows_left(CHUNKS // 2)
    for h in halves[1:]:
        for ox in range(1, n_x):
            pass_on(0, ox, h)
    for n in range(CHUNKS // 2 + 1, CHUNKS):
        rows_left(n)

    key = lax.broadcasted_iota(jnp.int32, (CB, KC * CB), 1)
    key = jnp.where(key % CB == lax.broadcasted_iota(jnp.int32, key.shape, 0), key // CB, -2)

    @pl.loop(0, rows, unroll=2)
    def _(i):
        for k in range(nbr):
            slot = jnp.where(live[k, i] != 0, slots[k, i], -1)
            sel[i, k * CB:(k + 1) * CB, :] = jnp.where(key == slot, 1.0, 0.0).astype(jnp.bfloat16)

    for h in halves:
        for dz in (-1, 1):
            pass_on(dz, 0, h)

    ce_copy.wait_recv()
    wide_ce = jnp.concatenate([jnp.broadcast_to(ce[h, :1], (CB, rows * CB)) for h in range(CORES)], axis=1)
    lane = lax.broadcasted_iota(jnp.int32, wide_ce.shape, 1)
    row = lax.broadcasted_iota(jnp.int32, wide_ce.shape, 0)
    wide_ce = jnp.where(lane % CB == row, wide_ce - (z - 1) * slab_coarse, -(2 ** 20))
    for g in range(3):
        for t in range(n_x):
            for q in range(ncr):
                pick = wide_ce == g * slab_coarse + (t * CORES + c) * ncr + q
                picks[g, t * piece + q * CB:t * piece + (q + 1) * CB, :] = (
                    jnp.where(pick, 1.0, 0.0).astype(jnp.bfloat16))

    for h in reversed(halves):
        for ox in range(1, n_x):
            for dz in (-1, 1):
                pass_on(dz, ox, h)
    for h in halves:
        for dz, ox in offsets:
            there(-dz, lambda dz=dz, ox=ox, h=h: fwd(dz, ox, 1 - c, h).wait_recv())

    first_row = (z - 1) * slab_rows
    lane_term = lax.broadcasted_iota(jnp.int32, (CB, nbr * CB), 1) // CB

    def right(i):
        far = jnp.concatenate(
            [wide[jnp.clip(columns[k, i] - first_row, 0, 3 * slab_rows - 1)] for k in range(nbr)], axis=0)
        every = lax.dot_general(qs[i], jnp.concatenate([far, far], axis=1), NT,
                                preferred_element_type=jnp.float32)
        term = every[:CB]
        for k in range(1, nbr):
            term = jnp.where(lane_term == k, every[k * CB:(k + 1) * CB], term)
        high = term.astype(jnp.bfloat16)
        low = (term - high.astype(jnp.float32)).astype(jnp.bfloat16)
        th[i, :CB] = high
        th[i, CB:] = low

    def put(i):
        placed = jnp.dot(th[i], sel[i], preferred_element_type=jnp.float32)
        tb[0, pl.ds(pl.multiple_of(i * CB, CB), CB), :] = (placed[:CB] + placed[CB:]).astype(jnp.bfloat16)

    each = rows // SHARES

    def share(n):
        at = pl.ds(n * each * CB, each * CB)
        return pltpu.make_async_remote_copy(
            src_ref=tb.at[0, at], dst_ref=tb.at[1, at], send_sem=ts.at[n], recv_sem=tr.at[n], **to_mate)

    @pl.loop(0, rows, unroll=16)
    def _(i):
        right(i)

    for n in range(SHARES):
        @pl.loop(0, each, unroll=each)
        def _(t):
            put(n * each + t)
        share(n).start()

    groups = (0, 2, 1)
    for g in groups:
        wo[g] = jnp.dot(picks[g, :, :rows * CB], tb[0], preferred_element_type=jnp.float32)
    for n in range(SHARES):
        share(n).wait_recv()

    def p2(dz, ox):
        at = pl.ds(pl.multiple_of(lax.rem(x + ox, n_x) * piece, piece), piece)
        return pltpu.make_async_remote_copy(
            src_ref=sb.at[dz + 1, at], dst_ref=rbuf.at[dz + 1, ox],
            send_sem=p2s.at[dz + 1, ox], recv_sem=p2r.at[dz + 1, ox],
            device_id={"slab": z + dz, "sub": to_sub(ox)}, device_id_type=MESH)

    for g in groups:
        sb[g] = (wo[g] + jnp.dot(picks[g, :, rows * CB:], tb[1], preferred_element_type=jnp.float32)).astype(jnp.bfloat16)
        for ox in reversed(range(n_x)):
            if (g - 1, ox) != (0, 0):
                there(g - 1, lambda dz=g - 1, ox=ox: p2(dz, ox).start())

    total = sb[1, pl.ds(pl.multiple_of(x * piece, piece), piece), :].astype(jnp.float32)
    for dz, ox in plane:
        there(-dz, lambda dz=dz, ox=ox: p2(dz, ox).wait_recv())
    for dz, ox in plane:
        total = total + rbuf[dz + 1, ox].astype(jnp.float32)
    out[...] = total.reshape(out.shape)

    ce_copy.wait_send()
    for n in range(SHARES):
        share(n).wait_send()
    for dz, ox in plane:
        there(dz, lambda dz=dz, ox=ox: p2(dz, ox).wait_send())
        for h in halves:
            there(dz, lambda dz=dz, ox=ox, h=h: p1_send(dz, ox, h).wait_send())
    for dz, ox in offsets:
        for h in halves:
            there(-dz, lambda dz=dz, ox=ox, h=h: fwd(dz, ox, c, h).wait_send())


def body(n_slab, n_sub, blocks, prolong, columns, live, slots, coarse_of):
    rows, nbr = blocks.shape[:2]
    ncr = rows // 4
    n_x = n_sub // CORES
    half = n_x * ncr * CB
    hbm = pl.BlockSpec(memory_space=pltpu.HBM)
    dma = pltpu.SemaphoreType.DMA
    flops = 2 * rows * nbr * CB * BS * (BS + CB)
    return pl.pallas_call(
        functools.partial(kernel, n_slab, n_sub),
        out_shape=jax.ShapeDtypeStruct((ncr, CB, KC * CB), jnp.float32),
        in_specs=[hbm] * 6,
        out_specs=pl.BlockSpec(memory_space=pltpu.VMEM),
        scratch_shapes=[
            pltpu.SMEM((nbr, rows), jnp.int32), pltpu.SMEM((nbr, rows), jnp.int32),
            pltpu.SMEM((nbr, rows), jnp.int32), pltpu.SMEM((rows,), jnp.int32),
            pltpu.VMEM((3 * n_sub * rows, CB, BS), jnp.bfloat16),
            pltpu.VMEM((rows, nbr, BS, BS), jnp.bfloat16),
            pltpu.VMEM((rows, nbr * CB, 2 * BS), jnp.bfloat16),
            pltpu.VMEM((rows, nbr * CB, KC * CB), jnp.bfloat16),
            pltpu.VMEM((rows, 2 * CB, nbr * CB), jnp.bfloat16),
            pltpu.VMEM((CORES, rows * CB, KC * CB), jnp.bfloat16),
            pltpu.VMEM((CORES, 8, rows * CB), jnp.int32),
            pltpu.VMEM((3, half, CORES * rows * CB), jnp.bfloat16),
            pltpu.VMEM((3, half, KC * CB), jnp.float32),
            pltpu.VMEM((3, half, KC * CB), jnp.bfloat16),
            pltpu.VMEM((3, n_x, ncr * CB, KC * CB), jnp.bfloat16),
            dma((4,)), dma(()), dma((CHUNKS,)),
            dma((3, n_x, HALVES)), dma((3, n_x, HALVES)), dma((3, n_x, HALVES)), dma((3, n_x, HALVES)),
            dma(()), dma(()), dma((SHARES,)), dma((SHARES,)), dma((3, n_x)), dma((3, n_x)),
        ],
        compiler_params=pltpu.CompilerParams(
            collective_id=0, has_side_effects=True, vmem_limit_bytes=63 * 2 ** 20),
        cost_estimate=pl.CostEstimate(flops=flops, bytes_accessed=2 * blocks.size, transcendentals=0),
    )(columns.T, live.T, slots.T, coarse_of, prolong, blocks)


def solution(mesh):
    rows = ("groups", "slab", "sub")
    in_specs = (
        P(rows, None, None, None), P(rows, None, None),
        P(rows, None), P(rows, None), P(rows, None), P(rows),
    )
    part = functools.partial(body, mesh.shape["slab"], mesh.shape["sub"])
    return jax.shard_map(part, mesh=mesh, in_specs=in_specs, out_specs=P(rows, None, None), check_vma=False)
```

```python
import functools

import jax
import jax.numpy as jnp
from jax import lax
from jax.experimental import pallas as pl
from jax.experimental.pallas import tpu as pltpu
from jax.sharding import PartitionSpec as P

BS = 128
CB = 32
KC = 8
CORES = 2
CHUNKS = 4
HALVES = 2
ALONG_X = 1
SHARES = 1
MESH = pl.DeviceIdType.MESH
NT = (((1,), (1,)), ((), ()))


def kernel(n_slab, n_sub, columns_in, live_in, slots_in, coarse_of_in, prolong, blocks, out,
           columns, live, slots, coarse_of, wide, blk, qs, sel, th, tb, ce, picks, wo, sb, rbuf,
           int_sem, own_sem, blk_sem, p1s, p1r, fs, fr, cs, cr, ts, tr, p2s, p2r):
    rows, nbr = blk.shape[0], blk.shape[1]
    n_x = n_sub // CORES
    ncr = rows // 4
    piece = ncr * CB
    slab_rows = rows * n_sub
    slab_coarse = ncr * n_sub
    z = lax.axis_index("slab")
    sub = lax.axis_index("sub")
    x, c = lax.div(sub, CORES), lax.rem(sub, CORES)
    mate = sub + 1 - 2 * c
    per = rows // CHUNKS
    to_mate = {"device_id": {"slab": z, "sub": mate}, "device_id_type": MESH}

    def there(dz, fn):
        if dz == 0:
            fn()
        else:
            pl.when(jnp.logical_and(z + dz >= 0, z + dz < n_slab))(fn)

    part = rows // HALVES

    def place(group, owner, h=None):
        first = (group * n_sub + owner) * rows
        return pl.ds(first, rows) if h is None else pl.ds(first + h * part, part)

    own = pltpu.make_async_copy(prolong, wide.at[place(1, sub)], own_sem)
    own.start()
    loads = [
        pltpu.make_async_copy(blocks.at[pl.ds(n * per, per)], blk.at[pl.ds(n * per, per)], blk_sem.at[n])
        for n in range(CHUNKS)
    ]
    for load in loads:
        load.start()
    ints = [
        pltpu.make_async_copy(given, kept, int_sem.at[n])
        for n, (given, kept) in enumerate(((coarse_of_in, coarse_of), (slots_in, slots), (live_in, live),
                                           (columns_in, columns)))
    ]
    for copy in ints:
        copy.start()

    barrier = pltpu.get_barrier_semaphore()
    offsets = [(dz, ox) for dz in (0, -1, 1) for ox in range(n_x)]
    plane = [o for o in offsets if o != (0, 0)]

    def to_sub(ox):
        return lax.rem(x + ox, n_x) * CORES + c

    def from_sub(ox, core):
        return lax.rem(x + n_x - ox, n_x) * CORES + core

    def greet(dz, ox):
        def go():
            pl.semaphore_signal(barrier, inc=1, device_id={"slab": z + dz, "sub": to_sub(ox)},
                                device_id_type=MESH)
        return go

    pl.semaphore_signal(barrier, inc=1, device_id={"sub": mate}, device_id_type=MESH)
    for dz, ox in plane:
        there(dz, greet(dz, ox))
    ends = (z == 0).astype(jnp.int32) + (z == n_slab - 1).astype(jnp.int32)
    pl.semaphore_wait(barrier, 3 * n_x - n_x * ends)

    def spot(dz, ox, core, h):
        return wide.at[place(1 - dz, from_sub(ox, core), h)]

    def last_x(dz, ox, h):
        return dz != 0 and ox != 0 and h >= HALVES - ALONG_X

    def p1_send(dz, ox, h):
        dst = wide.at[place(1 - dz, sub, h)]
        target = {"slab": z + dz, "sub": to_sub(ox)}
        if dz == 0 or ox == 0:
            src = prolong.at[pl.ds(h * part, part)]
        elif last_x(dz, ox, h):
            src, target = spot(dz, 0, c, h), {"slab": z, "sub": to_sub(ox)}
        else:
            src, dst, target = spot(0, ox, c, h), spot(dz, ox, c, h), {"slab": z + dz, "sub": sub}
        return pltpu.make_async_remote_copy(
            src_ref=src, dst_ref=dst,
            send_sem=p1s.at[dz + 1, ox, h], recv_sem=p1r.at[dz + 1, ox, h],
            device_id=target, device_id_type=MESH)

    def p1_recv(dz, ox, h):
        return pltpu.make_async_remote_copy(
            src_ref=spot(dz, ox, c, h), dst_ref=spot(dz, ox, c, h),
            send_sem=p1s.at[dz + 1, ox, h], recv_sem=p1r.at[dz + 1, ox, h], **to_mate)

    def fwd(dz, ox, core, h):
        return pltpu.make_async_remote_copy(
            src_ref=prolong.at[pl.ds(h * part, part)] if (dz, ox) == (0, 0) else spot(dz, ox, core, h),
            dst_ref=spot(dz, ox, core, h),
            send_sem=fs.at[dz + 1, ox, h], recv_sem=fr.at[dz + 1, ox, h], **to_mate)

    halves = range(HALVES)
    for h in halves:
        for ox in range(1, n_x):
            p1_send(0, ox, h).start()
        for dz in (-1, 1):
            there(dz, lambda dz=dz, h=HALVES - 1 - h: p1_send(dz, 0, h).start())
    for h in halves:
        fwd(0, 0, c, h).start()

    lane_row = lax.broadcasted_iota(jnp.int32, ce.shape[1:], 1) // CB
    mine = jnp.zeros(ce.shape[1:], jnp.int32)
    for copy in ints:
        copy.wait()
    for i in range(rows):
        mine = jnp.where(lane_row == i, coarse_of[i], mine)
    ce[0] = mine
    ce_copy = pltpu.make_async_remote_copy(
        src_ref=ce.at[0], dst_ref=ce.at[1], send_sem=cs, recv_sem=cr, **to_mate)
    ce_copy.start()

    for dz in (-1, 1):
        @pl.when(jnp.logical_not(jnp.logical_and(z - dz >= 0, z - dz < n_slab)))
        def _():
            rbuf[dz + 1] = jnp.zeros(rbuf.shape[1:], rbuf.dtype)

    own.wait()

    def left(i):
        mine = wide[(n_sub + sub) * rows + i]
        for k in range(nbr):
            q = jnp.dot(mine, blk[i, k], preferred_element_type=jnp.float32)
            high = q.astype(jnp.bfloat16)
            low = (q - high.astype(jnp.float32)).astype(jnp.bfloat16)
            qs[i, k * CB:(k + 1) * CB, :BS] = high
            qs[i, k * CB:(k + 1) * CB, BS:] = low

    def pass_on(dz, ox, h):
        def go():
            p1_recv(dz, ox, h).wait_recv()
            if dz == 0 and h < HALVES - ALONG_X:
                for to in (-1, 1):
                    there(to, lambda to=to: p1_send(to, ox, h).start())
            if ox == 0 and h >= HALVES - ALONG_X:
                for to in range(1, n_x):
                    p1_send(dz, to, h).start()
            fwd(dz, ox, c, h).start()
        there(-dz, go)

    def rows_left(n):
        loads[n].wait()

        @pl.loop(0, per, unroll=per)
        def _(t):
            left(n * per + t)

    for n in range(CHUNKS // 2):
        rows_left(n)
    for h in halves[:HALVES - ALONG_X]:
        for ox in range(1, n_x):
            pass_on(0, ox, h)
    for h in reversed(halves[HALVES - ALONG_X:]):
        for dz in (-1, 1):
            pass_on(dz, 0, h)
    rows_left(CHUNKS // 2)
    for h in halves[HALVES - ALONG_X:]:
        for ox in range(1, n_x):
            pass_on(0, ox, h)
    for n in range(CHUNKS // 2 + 1, CHUNKS):
        rows_left(n)

    key = lax.broadcasted_iota(jnp.int32, (CB, KC * CB), 1)
    key = jnp.where(key % CB == lax.broadcasted_iota(jnp.int32, key.shape, 0), key // CB, -2)

    @pl.loop(0, rows, unroll=2)
    def _(i):
        for k in range(nbr):
            slot = jnp.where(live[k, i] != 0, slots[k, i], -1)
            sel[i, k * CB:(k + 1) * CB, :] = jnp.where(key == slot, 1.0, 0.0).astype(jnp.bfloat16)

    for h in reversed(halves[:HALVES - ALONG_X]):
        for dz in (-1, 1):
            pass_on(dz, 0, h)

    ce_copy.wait_recv()
    wide_ce = jnp.concatenate([jnp.broadcast_to(ce[h, :1], (CB, rows * CB)) for h in range(CORES)], axis=1)
    lane = lax.broadcasted_iota(jnp.int32, wide_ce.shape, 1)
    row = lax.broadcasted_iota(jnp.int32, wide_ce.shape, 0)
    wide_ce = jnp.where(lane % CB == row, wide_ce - (z - 1) * slab_coarse, -(2 ** 20))
    for g in range(3):
        for t in range(n_x):
            for q in range(ncr):
                pick = wide_ce == g * slab_coarse + (t * CORES + c) * ncr + q
                picks[g, t * piece + q * CB:t * piece + (q + 1) * CB, :] = (
                    jnp.where(pick, 1.0, 0.0).astype(jnp.bfloat16))

    for h in halves:
        for ox in range(1, n_x):
            for dz in (-1, 1):
                pass_on(dz, ox, h)
    for h in halves:
        for dz, ox in offsets:
            there(-dz, lambda dz=dz, ox=ox, h=h: fwd(dz, ox, 1 - c, h).wait_recv())

    first_row = (z - 1) * slab_rows
    lane_term = lax.broadcasted_iota(jnp.int32, (CB, nbr * CB), 1) // CB

    def right(i):
        far = jnp.concatenate(
            [wide[jnp.clip(columns[k, i] - first_row, 0, 3 * slab_rows - 1)] for k in range(nbr)], axis=0)
        every = lax.dot_general(qs[i], jnp.concatenate([far, far], axis=1), NT,
                                preferred_element_type=jnp.float32)
        term = every[:CB]
        for k in range(1, nbr):
            term = jnp.where(lane_term == k, every[k * CB:(k + 1) * CB], term)
        high = term.astype(jnp.bfloat16)
        low = (term - high.astype(jnp.float32)).astype(jnp.bfloat16)
        th[i, :CB] = high
        th[i, CB:] = low

    def put(i):
        placed = jnp.dot(th[i], sel[i], preferred_element_type=jnp.float32)
        tb[0, pl.ds(pl.multiple_of(i * CB, CB), CB), :] = (placed[:CB] + placed[CB:]).astype(jnp.bfloat16)

    each = rows // SHARES

    def share(n):
        at = pl.ds(n * each * CB, each * CB)
        return pltpu.make_async_remote_copy(
            src_ref=tb.at[0, at], dst_ref=tb.at[1, at], send_sem=ts.at[n], recv_sem=tr.at[n], **to_mate)

    @pl.loop(0, rows, unroll=16)
    def _(i):
        right(i)

    for n in range(SHARES):
        @pl.loop(0, each, unroll=each)
        def _(t):
            put(n * each + t)
        share(n).start()

    groups = (0, 2, 1)
    for g in groups:
        wo[g] = jnp.dot(picks[g, :, :rows * CB], tb[0], preferred_element_type=jnp.float32)
    for n in range(SHARES):
        share(n).wait_recv()

    def p2(dz, ox):
        at = pl.ds(pl.multiple_of(lax.rem(x + ox, n_x) * piece, piece), piece)
        return pltpu.make_async_remote_copy(
            src_ref=sb.at[dz + 1, at], dst_ref=rbuf.at[dz + 1, ox],
            send_sem=p2s.at[dz + 1, ox], recv_sem=p2r.at[dz + 1, ox],
            device_id={"slab": z + dz, "sub": to_sub(ox)}, device_id_type=MESH)

    for g in groups:
        summed = wo[g] + jnp.dot(picks[g, :, rows * CB:], tb[1], preferred_element_type=jnp.float32)
        sb[g] = summed.astype(jnp.bfloat16)
        if g == 1:
            wo[g] = summed
        for ox in reversed(range(n_x)):
            if (g - 1, ox) != (0, 0):
                there(g - 1, lambda dz=g - 1, ox=ox: p2(dz, ox).start())

    total = wo[1, pl.ds(pl.multiple_of(x * piece, piece), piece), :]
    for dz, ox in plane:
        there(-dz, lambda dz=dz, ox=ox: p2(dz, ox).wait_recv())
    for dz, ox in plane:
        total = total + rbuf[dz + 1, ox].astype(jnp.float32)
    out[...] = total.reshape(out.shape)

    ce_copy.wait_send()
    for n in range(SHARES):
        share(n).wait_send()
    for dz, ox in plane:
        there(dz, lambda dz=dz, ox=ox: p2(dz, ox).wait_send())
        for h in halves:
            there(-dz if last_x(dz, ox, h) else dz,
                  lambda dz=dz, ox=ox, h=h: p1_send(dz, ox, h).wait_send())
    for dz, ox in offsets:
        for h in halves:
            there(-dz, lambda dz=dz, ox=ox, h=h: fwd(dz, ox, c, h).wait_send())


def body(n_slab, n_sub, blocks, prolong, columns, live, slots, coarse_of):
    rows, nbr = blocks.shape[:2]
    ncr = rows // 4
    n_x = n_sub // CORES
    half = n_x * ncr * CB
    hbm = pl.BlockSpec(memory_space=pltpu.HBM)
    dma = pltpu.SemaphoreType.DMA
    flops = 2 * rows * nbr * CB * BS * (BS + CB)
    return pl.pallas_call(
        functools.partial(kernel, n_slab, n_sub),
        out_shape=jax.ShapeDtypeStruct((ncr, CB, KC * CB), jnp.float32),
        in_specs=[hbm] * 6,
        out_specs=pl.BlockSpec(memory_space=pltpu.VMEM),
        scratch_shapes=[
            pltpu.SMEM((nbr, rows), jnp.int32), pltpu.SMEM((nbr, rows), jnp.int32),
            pltpu.SMEM((nbr, rows), jnp.int32), pltpu.SMEM((rows,), jnp.int32),
            pltpu.VMEM((3 * n_sub * rows, CB, BS), jnp.bfloat16),
            pltpu.VMEM((rows, nbr, BS, BS), jnp.bfloat16),
            pltpu.VMEM((rows, nbr * CB, 2 * BS), jnp.bfloat16),
            pltpu.VMEM((rows, nbr * CB, KC * CB), jnp.bfloat16),
            pltpu.VMEM((rows, 2 * CB, nbr * CB), jnp.bfloat16),
            pltpu.VMEM((CORES, rows * CB, KC * CB), jnp.bfloat16),
            pltpu.VMEM((CORES, 8, rows * CB), jnp.int32),
            pltpu.VMEM((3, half, CORES * rows * CB), jnp.bfloat16),
            pltpu.VMEM((3, half, KC * CB), jnp.float32),
            pltpu.VMEM((3, half, KC * CB), jnp.bfloat16),
            pltpu.VMEM((3, n_x, ncr * CB, KC * CB), jnp.bfloat16),
            dma((4,)), dma(()), dma((CHUNKS,)),
            dma((3, n_x, HALVES)), dma((3, n_x, HALVES)), dma((3, n_x, HALVES)), dma((3, n_x, HALVES)),
            dma(()), dma(()), dma((SHARES,)), dma((SHARES,)), dma((3, n_x)), dma((3, n_x)),
        ],
        compiler_params=pltpu.CompilerParams(
            collective_id=0, has_side_effects=True, vmem_limit_bytes=63 * 2 ** 20),
        cost_estimate=pl.CostEstimate(flops=flops, bytes_accessed=2 * blocks.size, transcendentals=0),
    )(columns.T, live.T, slots.T, coarse_of, prolong, blocks)


def solution(mesh):
    rows = ("groups", "slab", "sub")
    in_specs = (
        P(rows, None, None, None), P(rows, None, None),
        P(rows, None), P(rows, None), P(rows, None), P(rows),
    )
    part = functools.partial(body, mesh.shape["slab"], mesh.shape["sub"])
    return jax.shard_map(part, mesh=mesh, in_specs=in_specs, out_specs=P(rows, None, None), check_vma=False)
```

```python
import functools

import jax
import jax.numpy as jnp
from jax import lax
from jax.experimental import pallas as pl
from jax.experimental.pallas import tpu as pltpu
from jax.sharding import PartitionSpec as P

BS = 128
CB = 32
KC = 8
CORES = 2
CHUNKS = 4
HALVES = 2
ALONG_X = 1
SHARES = 1
MESH = pl.DeviceIdType.MESH
NT = (((1,), (1,)), ((), ()))


def kernel(n_slab, n_sub, columns_in, live_in, slots_in, coarse_of_in, prolong, blocks, out,
           columns, live, slots, coarse_of, wide, blk, qs, sel, th, tb, ce, picks, wo, sb, rbuf,
           int_sem, own_sem, blk_sem, p1s, p1r, fs, fr, cs, cr, ts, tr, p2s, p2r):
    rows, nbr = blk.shape[0], blk.shape[1]
    n_x = n_sub // CORES
    ncr = rows // 4
    piece = ncr * CB
    slab_rows = rows * n_sub
    slab_coarse = ncr * n_sub
    z = lax.axis_index("slab")
    sub = lax.axis_index("sub")
    x, c = lax.div(sub, CORES), lax.rem(sub, CORES)
    mate = sub + 1 - 2 * c
    per = rows // CHUNKS
    to_mate = {"device_id": {"slab": z, "sub": mate}, "device_id_type": MESH}

    def there(dz, fn):
        if dz == 0:
            fn()
        else:
            pl.when(jnp.logical_and(z + dz >= 0, z + dz < n_slab))(fn)

    part = rows // HALVES

    def place(group, owner, h=None):
        first = (group * n_sub + owner) * rows
        return pl.ds(first, rows) if h is None else pl.ds(first + h * part, part)

    own = pltpu.make_async_copy(prolong, wide.at[place(1, sub)], own_sem)
    own.start()
    loads = [
        pltpu.make_async_copy(blocks.at[pl.ds(n * per, per)], blk.at[pl.ds(n * per, per)], blk_sem.at[n])
        for n in range(CHUNKS)
    ]
    for load in loads:
        load.start()
    ints = [
        pltpu.make_async_copy(given, kept, int_sem.at[n])
        for n, (given, kept) in enumerate(((coarse_of_in, coarse_of), (slots_in, slots), (live_in, live),
                                           (columns_in, columns)))
    ]
    for copy in ints:
        copy.start()

    barrier = pltpu.get_barrier_semaphore()
    offsets = [(dz, ox) for dz in (0, -1, 1) for ox in range(n_x)]
    plane = [o for o in offsets if o != (0, 0)]

    def to_sub(ox):
        return lax.rem(x + ox, n_x) * CORES + c

    def from_sub(ox, core):
        return lax.rem(x + n_x - ox, n_x) * CORES + core

    def greet(dz, ox):
        def go():
            pl.semaphore_signal(barrier, inc=1, device_id={"slab": z + dz, "sub": to_sub(ox)},
                                device_id_type=MESH)
        return go

    pl.semaphore_signal(barrier, inc=1, device_id={"sub": mate}, device_id_type=MESH)
    for dz, ox in plane:
        if dz == 0 or ox == 0:
            there(dz, greet(dz, ox))
    ends = (z == 0).astype(jnp.int32) + (z == n_slab - 1).astype(jnp.int32)
    pl.semaphore_wait(barrier, n_x + 2 - ends)

    def spot(dz, ox, core, h):
        return wide.at[place(1 - dz, from_sub(ox, core), h)]

    def last_x(dz, ox, h):
        return dz != 0 and ox != 0 and h >= HALVES - ALONG_X

    def p1_send(dz, ox, h):
        dst = wide.at[place(1 - dz, sub, h)]
        target = {"slab": z + dz, "sub": to_sub(ox)}
        if dz == 0 or ox == 0:
            src = prolong.at[pl.ds(h * part, part)]
        elif last_x(dz, ox, h):
            src, target = spot(dz, 0, c, h), {"slab": z, "sub": to_sub(ox)}
        else:
            src, dst, target = spot(0, ox, c, h), spot(dz, ox, c, h), {"slab": z + dz, "sub": sub}
        return pltpu.make_async_remote_copy(
            src_ref=src, dst_ref=dst,
            send_sem=p1s.at[dz + 1, ox, h], recv_sem=p1r.at[dz + 1, ox, h],
            device_id=target, device_id_type=MESH)

    def p1_recv(dz, ox, h):
        return pltpu.make_async_remote_copy(
            src_ref=spot(dz, ox, c, h), dst_ref=spot(dz, ox, c, h),
            send_sem=p1s.at[dz + 1, ox, h], recv_sem=p1r.at[dz + 1, ox, h], **to_mate)

    def fwd(dz, ox, core, h):
        return pltpu.make_async_remote_copy(
            src_ref=prolong.at[pl.ds(h * part, part)] if (dz, ox) == (0, 0) else spot(dz, ox, core, h),
            dst_ref=spot(dz, ox, core, h),
            send_sem=fs.at[dz + 1, ox, h], recv_sem=fr.at[dz + 1, ox, h], **to_mate)

    halves = range(HALVES)
    for h in halves:
        for ox in range(1, n_x):
            p1_send(0, ox, h).start()
        for dz in (-1, 1):
            there(dz, lambda dz=dz, h=HALVES - 1 - h: p1_send(dz, 0, h).start())
    for h in halves:
        fwd(0, 0, c, h).start()

    lane_row = lax.broadcasted_iota(jnp.int32, ce.shape[1:], 1) // CB
    mine = jnp.zeros(ce.shape[1:], jnp.int32)
    for copy in ints:
        copy.wait()
    for i in range(rows):
        mine = jnp.where(lane_row == i, coarse_of[i], mine)
    ce[0] = mine
    ce_copy = pltpu.make_async_remote_copy(
        src_ref=ce.at[0], dst_ref=ce.at[1], send_sem=cs, recv_sem=cr, **to_mate)
    ce_copy.start()

    for dz in (-1, 1):
        @pl.when(jnp.logical_not(jnp.logical_and(z - dz >= 0, z - dz < n_slab)))
        def _():
            rbuf[dz + 1] = jnp.zeros(rbuf.shape[1:], rbuf.dtype)

    own.wait()

    def left(i):
        mine = wide[(n_sub + sub) * rows + i]
        for k in range(nbr):
            q = jnp.dot(mine, blk[i, k], preferred_element_type=jnp.float32)
            high = q.astype(jnp.bfloat16)
            low = (q - high.astype(jnp.float32)).astype(jnp.bfloat16)
            qs[i, k * CB:(k + 1) * CB, :BS] = high
            qs[i, k * CB:(k + 1) * CB, BS:] = low

    def pass_on(dz, ox, h):
        def go():
            p1_recv(dz, ox, h).wait_recv()
            if dz == 0 and h < HALVES - ALONG_X:
                for to in (-1, 1):
                    there(to, lambda to=to: p1_send(to, ox, h).start())
            if ox == 0 and h >= HALVES - ALONG_X:
                for to in range(1, n_x):
                    p1_send(dz, to, h).start()
            fwd(dz, ox, c, h).start()
        there(-dz, go)

    def rows_left(n):
        loads[n].wait()

        @pl.loop(0, per, unroll=per)
        def _(t):
            left(n * per + t)

    for n in range(CHUNKS // 2):
        rows_left(n)
    for h in halves[:HALVES - ALONG_X]:
        for ox in range(1, n_x):
            pass_on(0, ox, h)
    for h in reversed(halves[HALVES - ALONG_X:]):
        for dz in (-1, 1):
            pass_on(dz, 0, h)
    rows_left(CHUNKS // 2)
    for h in halves[HALVES - ALONG_X:]:
        for ox in range(1, n_x):
            pass_on(0, ox, h)
    for n in range(CHUNKS // 2 + 1, CHUNKS):
        rows_left(n)

    key = lax.broadcasted_iota(jnp.int32, (CB, KC * CB), 1)
    key = jnp.where(key % CB == lax.broadcasted_iota(jnp.int32, key.shape, 0), key // CB, -2)

    @pl.loop(0, rows, unroll=2)
    def _(i):
        for k in range(nbr):
            slot = jnp.where(live[k, i] != 0, slots[k, i], -1)
            sel[i, k * CB:(k + 1) * CB, :] = jnp.where(key == slot, 1.0, 0.0).astype(jnp.bfloat16)

    for h in reversed(halves[:HALVES - ALONG_X]):
        for dz in (-1, 1):
            pass_on(dz, 0, h)

    ce_copy.wait_recv()
    wide_ce = jnp.concatenate([jnp.broadcast_to(ce[h, :1], (CB, rows * CB)) for h in range(CORES)], axis=1)
    lane = lax.broadcasted_iota(jnp.int32, wide_ce.shape, 1)
    row = lax.broadcasted_iota(jnp.int32, wide_ce.shape, 0)
    wide_ce = jnp.where(lane % CB == row, wide_ce - (z - 1) * slab_coarse, -(2 ** 20))
    for g in range(3):
        for t in range(n_x):
            for q in range(ncr):
                pick = wide_ce == g * slab_coarse + (t * CORES + c) * ncr + q
                picks[g, t * piece + q * CB:t * piece + (q + 1) * CB, :] = (
                    jnp.where(pick, 1.0, 0.0).astype(jnp.bfloat16))

    for h in halves:
        for ox in range(1, n_x):
            for dz in (-1, 1):
                pass_on(dz, ox, h)
    for h in halves:
        for dz, ox in offsets:
            there(-dz, lambda dz=dz, ox=ox, h=h: fwd(dz, ox, 1 - c, h).wait_recv())

    first_row = (z - 1) * slab_rows
    lane_term = lax.broadcasted_iota(jnp.int32, (CB, nbr * CB), 1) // CB

    def right(i):
        far = jnp.concatenate(
            [wide[jnp.clip(columns[k, i] - first_row, 0, 3 * slab_rows - 1)] for k in range(nbr)], axis=0)
        every = lax.dot_general(qs[i], jnp.concatenate([far, far], axis=1), NT,
                                preferred_element_type=jnp.float32)
        term = every[:CB]
        for k in range(1, nbr):
            term = jnp.where(lane_term == k, every[k * CB:(k + 1) * CB], term)
        high = term.astype(jnp.bfloat16)
        low = (term - high.astype(jnp.float32)).astype(jnp.bfloat16)
        th[i, :CB] = high
        th[i, CB:] = low

    def put(i):
        placed = jnp.dot(th[i], sel[i], preferred_element_type=jnp.float32)
        tb[0, pl.ds(pl.multiple_of(i * CB, CB), CB), :] = (placed[:CB] + placed[CB:]).astype(jnp.bfloat16)

    each = rows // SHARES

    def share(n):
        at = pl.ds(n * each * CB, each * CB)
        return pltpu.make_async_remote_copy(
            src_ref=tb.at[0, at], dst_ref=tb.at[1, at], send_sem=ts.at[n], recv_sem=tr.at[n], **to_mate)

    @pl.loop(0, rows, unroll=16)
    def _(i):
        right(i)

    for n in range(SHARES):
        @pl.loop(0, each, unroll=each)
        def _(t):
            put(n * each + t)
        share(n).start()

    groups = (0, 2, 1)
    for g in groups:
        wo[g] = jnp.dot(picks[g, :, :rows * CB], tb[0], preferred_element_type=jnp.float32)
    for n in range(SHARES):
        share(n).wait_recv()

    def p2(dz, ox):
        at = pl.ds(pl.multiple_of(lax.rem(x + ox, n_x) * piece, piece), piece)
        return pltpu.make_async_remote_copy(
            src_ref=sb.at[dz + 1, at], dst_ref=rbuf.at[dz + 1, ox],
            send_sem=p2s.at[dz + 1, ox], recv_sem=p2r.at[dz + 1, ox],
            device_id={"slab": z + dz, "sub": to_sub(ox)}, device_id_type=MESH)

    for g in groups:
        summed = wo[g] + jnp.dot(picks[g, :, rows * CB:], tb[1], preferred_element_type=jnp.float32)
        sb[g] = summed.astype(jnp.bfloat16)
        if g == 1:
            wo[g] = summed
        for ox in reversed(range(n_x)):
            if (g - 1, ox) != (0, 0):
                there(g - 1, lambda dz=g - 1, ox=ox: p2(dz, ox).start())

    total = wo[1, pl.ds(pl.multiple_of(x * piece, piece), piece), :]
    for dz, ox in plane:
        there(-dz, lambda dz=dz, ox=ox: p2(dz, ox).wait_recv())
    for dz, ox in plane:
        total = total + rbuf[dz + 1, ox].astype(jnp.float32)
    out[...] = total.reshape(out.shape)

    ce_copy.wait_send()
    for n in range(SHARES):
        share(n).wait_send()
    for dz, ox in plane:
        there(dz, lambda dz=dz, ox=ox: p2(dz, ox).wait_send())
        for h in halves:
            there(-dz if last_x(dz, ox, h) else dz,
                  lambda dz=dz, ox=ox, h=h: p1_send(dz, ox, h).wait_send())
    for dz, ox in offsets:
        for h in halves:
            there(-dz, lambda dz=dz, ox=ox, h=h: fwd(dz, ox, c, h).wait_send())


def body(n_slab, n_sub, blocks, prolong, columns, live, slots, coarse_of):
    rows, nbr = blocks.shape[:2]
    ncr = rows // 4
    n_x = n_sub // CORES
    half = n_x * ncr * CB
    hbm = pl.BlockSpec(memory_space=pltpu.HBM)
    dma = pltpu.SemaphoreType.DMA
    flops = 2 * rows * nbr * CB * BS * (BS + CB)
    return pl.pallas_call(
        functools.partial(kernel, n_slab, n_sub),
        out_shape=jax.ShapeDtypeStruct((ncr, CB, KC * CB), jnp.float32),
        in_specs=[hbm] * 6,
        out_specs=pl.BlockSpec(memory_space=pltpu.VMEM),
        scratch_shapes=[
            pltpu.SMEM((nbr, rows), jnp.int32), pltpu.SMEM((nbr, rows), jnp.int32),
            pltpu.SMEM((nbr, rows), jnp.int32), pltpu.SMEM((rows,), jnp.int32),
            pltpu.VMEM((3 * n_sub * rows, CB, BS), jnp.bfloat16),
            pltpu.VMEM((rows, nbr, BS, BS), jnp.bfloat16),
            pltpu.VMEM((rows, nbr * CB, 2 * BS), jnp.bfloat16),
            pltpu.VMEM((rows, nbr * CB, KC * CB), jnp.bfloat16),
            pltpu.VMEM((rows, 2 * CB, nbr * CB), jnp.bfloat16),
            pltpu.VMEM((CORES, rows * CB, KC * CB), jnp.bfloat16),
            pltpu.VMEM((CORES, 8, rows * CB), jnp.int32),
            pltpu.VMEM((3, half, CORES * rows * CB), jnp.bfloat16),
            pltpu.VMEM((3, half, KC * CB), jnp.float32),
            pltpu.VMEM((3, half, KC * CB), jnp.bfloat16),
            pltpu.VMEM((3, n_x, ncr * CB, KC * CB), jnp.bfloat16),
            dma((4,)), dma(()), dma((CHUNKS,)),
            dma((3, n_x, HALVES)), dma((3, n_x, HALVES)), dma((3, n_x, HALVES)), dma((3, n_x, HALVES)),
            dma(()), dma(()), dma((SHARES,)), dma((SHARES,)), dma((3, n_x)), dma((3, n_x)),
        ],
        compiler_params=pltpu.CompilerParams(
            collective_id=0, has_side_effects=True, vmem_limit_bytes=63 * 2 ** 20),
        cost_estimate=pl.CostEstimate(flops=flops, bytes_accessed=2 * blocks.size, transcendentals=0),
    )(columns.T, live.T, slots.T, coarse_of, prolong, blocks)


def solution(mesh):
    rows = ("groups", "slab", "sub")
    in_specs = (
        P(rows, None, None, None), P(rows, None, None),
        P(rows, None), P(rows, None), P(rows, None), P(rows),
    )
    part = functools.partial(body, mesh.shape["slab"], mesh.shape["sub"])
    return jax.shard_map(part, mesh=mesh, in_specs=in_specs, out_specs=P(rows, None, None), check_vma=False)
```
